32 devices in a mesh: frag: 2 (over y), dev: 4 (over z), col: 4 (over x, core).
Axes of the slice: x: 2, y: 2, z: 4, core: 2. Of those that a mesh axis runs over, the one named last changes fastest.
Arguments:
- factor_ac: bfloat16 [3072, 32, 512], P(('frag', 'dev'), None, 'col'), parts along dimension 0, may hold values from -0.95703125 to 0.95703125
- factor_bd: bfloat16 [3072, 32, 512], P(('frag', 'col'), None, 'dev'), parts along dimension 0, may hold values from -0.95703125 to 0.95703125
- amplitudes: bfloat16 [1024, 512, 256], P(('frag', 'col'), 'dev'), parts along dimension 0, may hold values from -0.015625 to 0.015625
Outputs:
- ladder_residual: float32 [64, 32, 256], P(('frag', 'col'), 'dev'), parts along dimension 0
The draws below stay inside these ranges and needn't reach their ends.
There are 2 independent parts, one for each index of `frag`. The reference program is written for one: setup_inputs(seed, part) draws one part's arguments, and reference() takes and returns one part's arrays. A program takes and returns all parts, laid end to end along the dimension named above; each array names one. Nothing has to cross between parts.
All inputs are finite; a program needn't handle non-finite values.
Results may differ from the reference program's by a relative error of at most 0.0029.
Values may be sent and summed in bfloat16 or wider, within the bound.
A program may use at most 128 MiB of HBM per device.

```python
import jax
import jax.numpy as jnp
from jax import lax

NV = 512
NAUX = 1536
AW = 32
BW = 32
NPAIR = 256


def spiked(drawn, own_key, source, target, shards_of, factor):
    owner, partner = [(jnp.arange(drawn.shape[dim]) // (drawn.shape[dim] // shards_of)).reshape([-1 if axis == dim else 1 for axis in range(drawn.ndim)]) for dim in (source, target)]
    chosen = jax.random.permutation(own_key, shards_of)[partner]
    strong = (owner == chosen) | (owner == (partner + shards_of // 2) % shards_of)
    return jnp.where(strong, factor * drawn, drawn)


def steps_of(stream_key, extent, cuts, low, top_value):
    def one(position, parts):
        draws = jax.random.uniform(jax.random.fold_in(jax.random.fold_in(stream_key, 6), position), (parts,), jnp.float32, low / len(cuts), top_value / len(cuts))
        return jnp.repeat(jnp.exp(draws), extent[position] // parts).reshape((-1,) + (1,) * (len(extent) - position - 1))

    level = one(*cuts[0])
    for cut in cuts[1:]:
        level = level * one(*cut)
    return level


def centred(own_key, shape, scale, limit, cuts=(), dtype=jnp.bfloat16):
    gain = steps_of(own_key, shape, cuts, -0.22, 0.18) if cuts else 1.0
    result = jax.random.normal(own_key, shape, jnp.float32) * scale * gain
    return jnp.minimum(jnp.maximum(result, -limit), limit).astype(dtype)


def gaussian_with(stream_key, dims, deviation, reach, cuts, heavy, held_as=jnp.bfloat16):
    drawn = deviation * jax.random.normal(stream_key, dims, jnp.float32)
    if cuts:
        drawn = drawn * steps_of(stream_key, dims, cuts, -0.22, 0.18)
    return jnp.clip(spiked(drawn, jax.random.fold_in(stream_key, 3), *heavy), -reach, reach).astype(held_as)


def setup_inputs(seed: int = 0, part: int = 0) -> dict:
    key_of = jax.random.split(jax.random.key(seed), 4)
    part_keys = jax.random.split(jax.random.fold_in(key_of[3], part), 4)
    return {
        "factor_ac": centred(part_keys[0], (NAUX, AW, NV), (NAUX ** -0.25), 0.95703125, ((0, 4), (2, 4))),
        "factor_bd": centred(part_keys[1], (NAUX, BW, NV), (NAUX ** -0.25), 0.95703125, ((0, 4), (2, 4))),
        "amplitudes": gaussian_with(part_keys[2], (NV, NV, NPAIR), (NV * NV) ** -0.5, 0.015625, ((0, 4), (1, 4)), (1, 2, 4, 2.0)),
    }


def reference(factor_ac, factor_bd, amplitudes):
    left = factor_ac.astype(jnp.float32)
    right = factor_bd.astype(jnp.float32)
    amps = amplitudes.astype(jnp.float32)
    width = NV // 8
    total = jnp.zeros((AW, BW, NPAIR), jnp.float32)
    for block in range(8):
        part_bd = right[:, :, block * width:(block + 1) * width]
        integral = jnp.einsum('qac,qbd->abdc', left, part_bd).astype(jnp.bfloat16)
        integral = lax.optimization_barrier(integral).astype(jnp.float32)
        part_amps = amps[:, block * width:(block + 1) * width, :]
        total = total + jnp.einsum('abdc,cdp->abp', integral, part_amps)
    return total
```

```python
import functools

import jax
import jax.numpy as jnp
from jax import lax
from jax.experimental import pallas as pl
from jax.experimental.pallas import tpu as pltpu
from jax.sharding import PartitionSpec as P

MESH = pl.DeviceIdType.MESH
CHUNKS = 8
PIECES = 4
AHEAD = 3
NT = 512


def kernel(nz, aw, dw, cw, ac_ref, bd_ref, t_ref, out_ref, ac_all, bd_all, t_all, x_buf,
           load_sem, bd_send, bd_recv, fw_send, fw_recv, send_r, recv_r, send_l, recv_l):
    z = lax.axis_index("dev")
    me = lax.axis_index("col")
    sib = me + 1 - 2 * lax.rem(me, 2)
    far = lax.rem(me + 2, 4)
    farsib = lax.rem(sib + 2, 4)
    has_r, has_l = z < nz - 1, z > 0
    rows_total, qz = ac_ref.shape
    qc, n_total = bd_ref.shape
    rows = rows_total // CHUNKS
    part = qc // PIECES
    hops = nz - 1

    barrier = pltpu.get_barrier_semaphore()
    for peer in (sib, far):
        pl.semaphore_signal(barrier, inc=1, device_id={"col": peer}, device_id_type=MESH)

    @pl.when(has_r)
    def _():
        pl.semaphore_signal(barrier, inc=1, device_id={"dev": z + 1}, device_id_type=MESH)

    @pl.when(has_l)
    def _():
        pl.semaphore_signal(barrier, inc=1, device_id={"dev": z - 1}, device_id_type=MESH)

    pl.semaphore_wait(barrier, 2 + has_r.astype(jnp.int32) + has_l.astype(jnp.int32))

    def ac_slot(j, k):
        return ac_all.at[pl.ds(pl.multiple_of(k * rows, rows), rows),
                         pl.ds(pl.multiple_of(j * qz, qz), qz)]

    def own(k):
        return ac_ref.at[pl.ds(pl.multiple_of(k * rows, rows), rows), :]

    def right(h, k):
        j = z - h
        return pltpu.make_async_remote_copy(
            src_ref=own(k) if h == 0 else ac_slot(j, k), dst_ref=ac_slot(j, k),
            send_sem=send_r.at[h, k], recv_sem=recv_r.at[h, k],
            device_id={"dev": z + 1}, device_id_type=MESH)

    def left(h, k):
        j = z + h
        return pltpu.make_async_remote_copy(
            src_ref=own(k) if h == 0 else ac_slot(j, k), dst_ref=ac_slot(j, k),
            send_sem=send_l.at[h, k], recv_sem=recv_l.at[h, k],
            device_id={"dev": z - 1}, device_id_type=MESH)

    def from_left(h, k):
        j = z - 1 - h
        return pltpu.make_async_remote_copy(
            src_ref=ac_slot(j, k), dst_ref=ac_slot(j, k),
            send_sem=send_r.at[h, k], recv_sem=recv_r.at[h, k],
            device_id={"dev": z - 1}, device_id_type=MESH)

    def from_right(h, k):
        j = z + 1 + h
        return pltpu.make_async_remote_copy(
            src_ref=ac_slot(j, k), dst_ref=ac_slot(j, k),
            send_sem=send_l.at[h, k], recv_sem=recv_l.at[h, k],
            device_id={"dev": z + 1}, device_id_type=MESH)

    def send_own(k):
        @pl.when(has_r)
        def _():
            right(0, k).start()

        @pl.when(has_l)
        def _():
            left(0, k).start()

    def bd_slot(j, p):
        return bd_all.at[pl.ds(pl.multiple_of(j * qc + p * part, part), part), :]

    def bd_own(p):
        return bd_ref.at[pl.ds(p * part, part), :]

    def bd_copy(way, j, p, peer, own_src):
        ss, rs = (fw_send, fw_recv) if way == 2 else (bd_send.at[way], bd_recv.at[way])
        return pltpu.make_async_remote_copy(
            src_ref=bd_own(p) if own_src else bd_slot(j, p), dst_ref=bd_slot(j, p),
            send_sem=ss.at[p], recv_sem=rs.at[p],
            device_id={"col": peer}, device_id_type=MESH)

    for p in range(PIECES):
        bd_copy(0, me, p, far, True).start()
    for k in range(AHEAD):
        send_own(k)
    for p in range(PIECES):
        bd_copy(1, me, p, sib, True).start()
    loads = [
        pltpu.make_async_copy(bd_ref, bd_all.at[pl.ds(pl.multiple_of(me * qc, qc), qc), :], load_sem.at[0]),
        pltpu.make_async_copy(ac_ref, ac_all.at[:, pl.ds(pl.multiple_of(z * qz, qz), qz)], load_sem.at[1]),
        pltpu.make_async_copy(t_ref, t_all, load_sem.at[2]),
    ]
    for copy in loads:
        copy.start()
    out_ref[...] = jnp.zeros_like(out_ref)

    def pump(h, k):
        @pl.when(z - 1 - h >= 0)
        def _():
            from_left(h, k).wait_recv()
            if h + 1 < hops:
                @pl.when(has_r)
                def _():
                    right(h + 1, k).start()

        @pl.when(z + 1 + h < nz)
        def _():
            from_right(h, k).wait_recv()
            if h + 1 < hops:
                @pl.when(has_l)
                def _():
                    left(h + 1, k).start()

    def compute(k):
        first = pl.multiple_of(k * rows, rows)
        c_in = rows // aw
        b_in = NT // dw

        def tile(n, carry):
            block = jnp.dot(
                ac_all[pl.ds(first, rows), :],
                bd_all[:, pl.ds(pl.multiple_of(n * NT, NT), NT)],
                preferred_element_type=jnp.float32,
            ).astype(jnp.bfloat16)
            for b in range(b_in):
                at = pl.multiple_of((n * b_in + b) * aw, aw)
                for c in range(c_in):
                    x_buf[pl.ds(at, aw), c * dw:(c + 1) * dw] = (
                        block[c * aw:(c + 1) * aw, b * dw:(b + 1) * dw])
            return carry

        lax.fori_loop(0, n_total // NT, tile, 0)
        kk = c_in * dw
        m = 256

        def add(i, carry):
            at = pl.ds(pl.multiple_of(i * m, m), m)
            out_ref[at, :] += jnp.dot(
                x_buf[at, :], t_all[pl.ds(pl.multiple_of(k * kk, kk), kk), :],
                preferred_element_type=jnp.float32)
            return carry

        lax.fori_loop(0, out_ref.shape[0] // m, add, 0)

    def step(s, carry):
        @pl.when(s + AHEAD < CHUNKS)
        def _():
            send_own(s + AHEAD)

        for h in range(hops):
            @pl.when((s >= h) & (s - h < CHUNKS))
            def _():
                pump(h, s - h)

        @pl.when(s == hops - 1)
        def _():
            for p in range(PIECES):
                bd_copy(0, far, p, far, False).wait_recv()
                bd_copy(2, far, p, sib, False).start()
            for p in range(PIECES):
                bd_copy(1, sib, p, sib, False).wait_recv()
            for p in range(PIECES):
                bd_copy(2, farsib, p, sib, False).wait_recv()
            for copy in loads:
                copy.wait()

        @pl.when(s >= hops - 1)
        def _():
            compute(s - (hops - 1))

        return carry

    lax.fori_loop(0, CHUNKS + hops - 1, step, 0)

    for p in range(PIECES):
        bd_copy(0, me, p, far, True).wait_send()
        bd_copy(1, me, p, sib, True).wait_send()
        bd_copy(2, far, p, sib, False).wait_send()

    def drain(k, carry):
        for h in range(hops):
            @pl.when(has_r & (z - h >= 0))
            def _():
                right(h, k).wait_send()

            @pl.when(has_l & (z + h < nz))
            def _():
                left(h, k).wait_send()
        return carry

    lax.fori_loop(0, CHUNKS, drain, 0)


def fused(nz, factor_ac, factor_bd, amplitudes):
    qz, aw, cw = factor_ac.shape
    qc, bw, dw = factor_bd.shape
    npair = amplitudes.shape[2]
    rows_ac = factor_ac.transpose(2, 1, 0).reshape(cw * aw, qz)
    rows_bd = factor_bd.reshape(qc, bw * dw)
    rows_t = amplitudes.reshape(cw * dw, npair)
    hops = nz - 1
    dma = pltpu.SemaphoreType.DMA
    any_space = pl.BlockSpec(memory_space=pl.ANY)
    partial_sum = pl.pallas_call(
        functools.partial(kernel, nz, aw, dw, cw),
        out_shape=jax.ShapeDtypeStruct((bw * aw, npair), jnp.float32),
        in_specs=[any_space] * 3,
        out_specs=pl.BlockSpec(memory_space=pltpu.VMEM),
        scratch_shapes=[
            pltpu.VMEM((cw * aw, nz * qz), jnp.bfloat16),
            pltpu.VMEM((4 * qc, bw * dw), jnp.bfloat16),
            pltpu.VMEM((cw * dw, npair), jnp.bfloat16),
            pltpu.VMEM((bw * aw, cw // CHUNKS * dw), jnp.bfloat16),
            dma((3,)), dma((2, PIECES)), dma((2, PIECES)), dma((PIECES,)), dma((PIECES,)),
            dma((hops, CHUNKS)), dma((hops, CHUNKS)), dma((hops, CHUNKS)), dma((hops, CHUNKS)),
        ],
        compiler_params=pltpu.CompilerParams(
            collective_id=0, has_side_effects=True, vmem_limit_bytes=58 * 2 ** 20),
    )(rows_ac, rows_bd, rows_t)
    partial_sum = partial_sum.reshape(bw, aw, npair)
    reduced = lax.psum_scatter(partial_sum, "col", scatter_dimension=1, tiled=True)
    result = lax.psum_scatter(reduced, "dev", scatter_dimension=0, tiled=True)
    return result.transpose(1, 0, 2)


def gathered(factor_ac, factor_bd, amplitudes):
    whole_bd = lax.all_gather(factor_bd, "col", axis=0, tiled=True)
    whole_ac = lax.all_gather(factor_ac, "dev", axis=0, tiled=True)
    integral = jnp.einsum("qac,qbd->abdc", whole_ac, whole_bd, preferred_element_type=jnp.float32)
    integral = integral.astype(jnp.bfloat16)
    partial_sum = jnp.einsum(
        "abdc,cdp->abp", integral, amplitudes, preferred_element_type=jnp.float32
    )
    reduced = lax.psum_scatter(partial_sum, "col", scatter_dimension=0, tiled=True)
    return lax.psum_scatter(reduced, "dev", scatter_dimension=1, tiled=True)


def solution(mesh):
    nz, ncol = mesh.shape["dev"], mesh.shape["col"]

    def local(factor_ac, factor_bd, amplitudes):
        qz, aw, cw = factor_ac.shape
        qc, bw, dw = factor_bd.shape
        held = 2 * (cw * aw * nz * qz + ncol * qc * bw * dw + cw * dw * amplitudes.shape[2])
        fits = (ncol == 4 and 2 <= nz and dw == 128 and qz % 128 == 0 and qc % (16 * PIECES) == 0
                and aw % 16 == 0 and cw % CHUNKS == 0 and bw * dw % NT == 0
                and bw * aw % 256 == 0 and CHUNKS >= AHEAD and held <= 36 * 2 ** 20)
        if fits:
            return fused(nz, factor_ac, factor_bd, amplitudes)
        return gathered(factor_ac, factor_bd, amplitudes)

    placed = (
        P(("frag", "dev"), None, "col"),
        P(("frag", "col"), None, "dev"),
        P(("frag", "col"), "dev", None),
    )
    return jax.shard_map(
        local,
        mesh=mesh,
        in_specs=placed,
        out_specs=P(("frag", "col"), "dev", None),
        check_vma=False,
    )
```

```python
import functools

import jax
import jax.numpy as jnp
from jax import lax
from jax.experimental import pallas as pl
from jax.experimental.pallas import tpu as pltpu
from jax.sharding import PartitionSpec as P

MESH = pl.DeviceIdType.MESH
CHUNKS = 8
PIECES = 4
AHEAD = 3
NT = 512


def kernel(nz, aw, dw, cw, ac_ref, bd_ref, t_ref, out_ref, ac_all, bd_all, t_all, x_buf,
           load_sem, bd_send, bd_recv, fw_send, fw_recv, send_r, recv_r, send_l, recv_l):
    z = lax.axis_index("dev")
    me = lax.axis_index("col")
    sib = me + 1 - 2 * lax.rem(me, 2)
    far = lax.rem(me + 2, 4)
    farsib = lax.rem(sib + 2, 4)
    has_r, has_l = z < nz - 1, z > 0
    rows_total, qz = ac_ref.shape
    qc, n_total = bd_ref.shape
    rows = rows_total // CHUNKS
    part = qc // PIECES
    hops = nz - 1

    barrier = pltpu.get_barrier_semaphore()
    for peer in (sib, far):
        pl.semaphore_signal(barrier, inc=1, device_id={"col": peer}, device_id_type=MESH)

    @pl.when(has_r)
    def _():
        pl.semaphore_signal(barrier, inc=1, device_id={"dev": z + 1}, device_id_type=MESH)

    @pl.when(has_l)
    def _():
        pl.semaphore_signal(barrier, inc=1, device_id={"dev": z - 1}, device_id_type=MESH)

    pl.semaphore_wait(barrier, 2 + has_r.astype(jnp.int32) + has_l.astype(jnp.int32))

    def ac_slot(j, k):
        return ac_all.at[pl.ds(pl.multiple_of(k * rows, rows), rows),
                         pl.ds(pl.multiple_of(j * qz, qz), qz)]

    def own(k):
        return ac_ref.at[pl.ds(pl.multiple_of(k * rows, rows), rows), :]

    def right(h, k):
        j = z - h
        return pltpu.make_async_remote_copy(
            src_ref=own(k) if h == 0 else ac_slot(j, k), dst_ref=ac_slot(j, k),
            send_sem=send_r.at[h, k], recv_sem=recv_r.at[h, k],
            device_id={"dev": z + 1}, device_id_type=MESH)

    def left(h, k):
        j = z + h
        return pltpu.make_async_remote_copy(
            src_ref=own(k) if h == 0 else ac_slot(j, k), dst_ref=ac_slot(j, k),
            send_sem=send_l.at[h, k], recv_sem=recv_l.at[h, k],
            device_id={"dev": z - 1}, device_id_type=MESH)

    def from_left(h, k):
        j = z - 1 - h
        return pltpu.make_async_remote_copy(
            src_ref=ac_slot(j, k), dst_ref=ac_slot(j, k),
            send_sem=send_r.at[h, k], recv_sem=recv_r.at[h, k],
            device_id={"dev": z - 1}, device_id_type=MESH)

    def from_right(h, k):
        j = z + 1 + h
        return pltpu.make_async_remote_copy(
            src_ref=ac_slot(j, k), dst_ref=ac_slot(j, k),
            send_sem=send_l.at[h, k], recv_sem=recv_l.at[h, k],
            device_id={"dev": z + 1}, device_id_type=MESH)

    def send_own(k):
        @pl.when(has_r)
        def _():
            right(0, k).start()

        @pl.when(has_l)
        def _():
            left(0, k).start()

    def bd_slot(j, p):
        return bd_all.at[pl.ds(pl.multiple_of(j * qc + p * part, part), part), :]

    def bd_own(p):
        return bd_ref.at[pl.ds(p * part, part), :]

    def bd_copy(way, j, p, peer, own_src):
        ss, rs = (fw_send, fw_recv) if way == 2 else (bd_send.at[way], bd_recv.at[way])
        return pltpu.make_async_remote_copy(
            src_ref=bd_own(p) if own_src else bd_slot(j, p), dst_ref=bd_slot(j, p),
            send_sem=ss.at[p], recv_sem=rs.at[p],
            device_id={"col": peer}, device_id_type=MESH)

    for p in range(PIECES):
        bd_copy(0, me, p, far, True).start()
    for k in range(AHEAD):
        send_own(k)
    for p in range(PIECES):
        bd_copy(1, me, p, sib, True).start()
    loads = [
        pltpu.make_async_copy(bd_ref, bd_all.at[pl.ds(pl.multiple_of(me * qc, qc), qc), :], load_sem.at[0]),
        pltpu.make_async_copy(ac_ref, ac_all.at[:, pl.ds(pl.multiple_of(z * qz, qz), qz)], load_sem.at[1]),
        pltpu.make_async_copy(t_ref, t_all, load_sem.at[2]),
    ]
    for copy in loads:
        copy.start()
    out_ref[...] = jnp.zeros_like(out_ref)

    def pump(h, k):
        @pl.when(z - 1 - h >= 0)
        def _():
            from_left(h, k).wait_recv()
            if h + 1 < hops:
                @pl.when(has_r)
                def _():
                    right(h + 1, k).start()

        @pl.when(z + 1 + h < nz)
        def _():
            from_right(h, k).wait_recv()
            if h + 1 < hops:
                @pl.when(has_l)
                def _():
                    left(h + 1, k).start()

    def compute(k):
        first = pl.multiple_of(k * rows, rows)
        c_in = rows // aw
        b_in = NT // dw

        def tile(n, carry):
            block = jnp.dot(
                ac_all[pl.ds(first, rows), :],
                bd_all[:, pl.ds(pl.multiple_of(n * NT, NT), NT)],
                preferred_element_type=jnp.float32,
            ).astype(jnp.bfloat16)
            for b in range(b_in):
                at = pl.multiple_of((n * b_in + b) * aw, aw)
                for c in range(c_in):
                    x_buf[pl.ds(at, aw), c * dw:(c + 1) * dw] = (
                        block[c * aw:(c + 1) * aw, b * dw:(b + 1) * dw])
            return carry

        lax.fori_loop(0, n_total // NT, tile, 0)
        kk = c_in * dw
        m = 256

        def add(i, carry):
            at = pl.ds(pl.multiple_of(i * m, m), m)
            out_ref[at, :] += jnp.dot(
                x_buf[at, :], t_all[pl.ds(pl.multiple_of(k * kk, kk), kk), :],
                preferred_element_type=jnp.float32)
            return carry

        lax.fori_loop(0, out_ref.shape[0] // m, add, 0)

    def step(s, carry):
        @pl.when(s + AHEAD < CHUNKS)
        def _():
            send_own(s + AHEAD)

        for h in range(hops):
            @pl.when((s >= h) & (s - h < CHUNKS))
            def _():
                pump(h, s - h)

        @pl.when(s == hops - 1)
        def _():
            for p in range(PIECES):
                bd_copy(0, far, p, far, False).wait_recv()
                bd_copy(2, far, p, sib, False).start()
            for p in range(PIECES):
                bd_copy(1, sib, p, sib, False).wait_recv()
            for p in range(PIECES):
                bd_copy(2, farsib, p, sib, False).wait_recv()
            for copy in loads:
                copy.wait()

        @pl.when(s >= hops - 1)
        def _():
            compute(s - (hops - 1))

        return carry

    lax.fori_loop(0, CHUNKS + hops - 1, step, 0)

    for p in range(PIECES):
        bd_copy(0, me, p, far, True).wait_send()
        bd_copy(1, me, p, sib, True).wait_send()
        bd_copy(2, far, p, sib, False).wait_send()

    def drain(k, carry):
        for h in range(hops):
            @pl.when(has_r & (z - h >= 0))
            def _():
                right(h, k).wait_send()

            @pl.when(has_l & (z + h < nz))
            def _():
                left(h, k).wait_send()
        return carry

    lax.fori_loop(0, CHUNKS, drain, 0)


def fused(nz, factor_ac, factor_bd, amplitudes):
    qz, aw, cw = factor_ac.shape
    qc, bw, dw = factor_bd.shape
    npair = amplitudes.shape[2]
    rows_ac = factor_ac.transpose(2, 1, 0).reshape(cw * aw, qz)
    rows_bd = factor_bd.reshape(qc, bw * dw)
    rows_t = amplitudes.reshape(cw * dw, npair)
    hops = nz - 1
    dma = pltpu.SemaphoreType.DMA
    any_space = pl.BlockSpec(memory_space=pl.ANY)
    partial_sum = pl.pallas_call(
        functools.partial(kernel, nz, aw, dw, cw),
        out_shape=jax.ShapeDtypeStruct((bw * aw, npair), jnp.float32),
        in_specs=[any_space] * 3,
        out_specs=pl.BlockSpec(memory_space=pltpu.VMEM),
        scratch_shapes=[
            pltpu.VMEM((cw * aw, nz * qz), jnp.bfloat16),
            pltpu.VMEM((4 * qc, bw * dw), jnp.bfloat16),
            pltpu.VMEM((cw * dw, npair), jnp.bfloat16),
            pltpu.VMEM((bw * aw, cw // CHUNKS * dw), jnp.bfloat16),
            dma((3,)), dma((2, PIECES)), dma((2, PIECES)), dma((PIECES,)), dma((PIECES,)),
            dma((hops, CHUNKS)), dma((hops, CHUNKS)), dma((hops, CHUNKS)), dma((hops, CHUNKS)),
        ],
        compiler_params=pltpu.CompilerParams(
            collective_id=0, has_side_effects=True, vmem_limit_bytes=58 * 2 ** 20),
    )(rows_ac, rows_bd, rows_t)
    blocks = partial_sum.reshape(nz, bw // nz, 4, aw // 4, npair).transpose(2, 0, 3, 1, 4)
    blocks = blocks.reshape(4 * nz, aw // 4, bw // nz, npair)
    return lax.all_to_all(blocks, ("col", "dev"), 0, 0, tiled=True).sum(0)


def gathered(factor_ac, factor_bd, amplitudes):
    whole_bd = lax.all_gather(factor_bd, "col", axis=0, tiled=True)
    whole_ac = lax.all_gather(factor_ac, "dev", axis=0, tiled=True)
    integral = jnp.einsum("qac,qbd->abdc", whole_ac, whole_bd, preferred_element_type=jnp.float32)
    integral = integral.astype(jnp.bfloat16)
    partial_sum = jnp.einsum(
        "abdc,cdp->abp", integral, amplitudes, preferred_element_type=jnp.float32
    )
    reduced = lax.psum_scatter(partial_sum, "col", scatter_dimension=0, tiled=True)
    return lax.psum_scatter(reduced, "dev", scatter_dimension=1, tiled=True)


def solution(mesh):
    nz, ncol = mesh.shape["dev"], mesh.shape["col"]

    def local(factor_ac, factor_bd, amplitudes):
        qz, aw, cw = factor_ac.shape
        qc, bw, dw = factor_bd.shape
        held = 2 * (cw * aw * nz * qz + ncol * qc * bw * dw + cw * dw * amplitudes.shape[2])
        fits = (ncol == 4 and 2 <= nz and dw == 128 and qz % 128 == 0 and qc % (16 * PIECES) == 0
                and aw % 16 == 0 and bw % nz == 0 and cw % CHUNKS == 0 and bw * dw % NT == 0
                and bw * aw % 256 == 0 and CHUNKS >= AHEAD and held <= 36 * 2 ** 20)
        if fits:
            return fused(nz, factor_ac, factor_bd, amplitudes)
        return gathered(factor_ac, factor_bd, amplitudes)

    placed = (
        P(("frag", "dev"), None, "col"),
        P(("frag", "col"), None, "dev"),
        P(("frag", "col"), "dev", None),
    )
    return jax.shard_map(
        local,
        mesh=mesh,
        in_specs=placed,
        out_specs=P(("frag", "col"), "dev", None),
        check_vma=False,
    )
```

```python
import functools

import jax
import jax.numpy as jnp
from jax import lax
from jax.experimental import pallas as pl
from jax.experimental.pallas import tpu as pltpu
from jax.sharding import PartitionSpec as P

MESH = pl.DeviceIdType.MESH
CHUNKS = 8
PIECES = 4
AHEAD = 3
NT = 1024


def kernel(nz, aw, dw, cw, ac_ref, bd_ref, t_ref, out_ref, ac_all, bd_all, t_all, x_buf, total,
           load_sem, bd_send, bd_recv, fw_send, fw_recv, send_r, recv_r, send_l, recv_l):
    z = lax.axis_index("dev")
    me = lax.axis_index("col")
    sib = me + 1 - 2 * lax.rem(me, 2)
    far = lax.rem(me + 2, 4)
    farsib = lax.rem(sib + 2, 4)
    has_r, has_l = z < nz - 1, z > 0
    rows_total, qz = ac_ref.shape
    qc, n_total = bd_ref.shape
    rows = rows_total // CHUNKS
    part = qc // PIECES
    hops = nz - 1

    barrier = pltpu.get_barrier_semaphore()
    for peer in (sib, far):
        pl.semaphore_signal(barrier, inc=1, device_id={"col": peer}, device_id_type=MESH)

    @pl.when(has_r)
    def _():
        pl.semaphore_signal(barrier, inc=1, device_id={"dev": z + 1}, device_id_type=MESH)

    @pl.when(has_l)
    def _():
        pl.semaphore_signal(barrier, inc=1, device_id={"dev": z - 1}, device_id_type=MESH)

    pl.semaphore_wait(barrier, 2 + has_r.astype(jnp.int32) + has_l.astype(jnp.int32))

    def ac_slot(j, k):
        return ac_all.at[pl.ds(pl.multiple_of(k * rows, rows), rows),
                         pl.ds(pl.multiple_of(j * qz, qz), qz)]

    def own(k):
        return ac_ref.at[pl.ds(pl.multiple_of(k * rows, rows), rows), :]

    def right(h, k):
        j = z - h
        return pltpu.make_async_remote_copy(
            src_ref=own(k) if h == 0 else ac_slot(j, k), dst_ref=ac_slot(j, k),
            send_sem=send_r.at[h, k], recv_sem=recv_r.at[h, k],
            device_id={"dev": z + 1}, device_id_type=MESH)

    def left(h, k):
        j = z + h
        return pltpu.make_async_remote_copy(
            src_ref=own(k) if h == 0 else ac_slot(j, k), dst_ref=ac_slot(j, k),
            send_sem=send_l.at[h, k], recv_sem=recv_l.at[h, k],
            device_id={"dev": z - 1}, device_id_type=MESH)

    def from_left(h, k):
        j = z - 1 - h
        return pltpu.make_async_remote_copy(
            src_ref=ac_slot(j, k), dst_ref=ac_slot(j, k),
            send_sem=send_r.at[h, k], recv_sem=recv_r.at[h, k],
            device_id={"dev": z - 1}, device_id_type=MESH)

    def from_right(h, k):
        j = z + 1 + h
        return pltpu.make_async_remote_copy(
            src_ref=ac_slot(j, k), dst_ref=ac_slot(j, k),
            send_sem=send_l.at[h, k], recv_sem=recv_l.at[h, k],
            device_id={"dev": z + 1}, device_id_type=MESH)

    def send_own(k):
        @pl.when(has_r)
        def _():
            right(0, k).start()

        @pl.when(has_l)
        def _():
            left(0, k).start()

    def bd_slot(j, p):
        return bd_all.at[pl.ds(pl.multiple_of(j * qc + p * part, part), part), :]

    def bd_own(p):
        return bd_ref.at[pl.ds(p * part, part), :]

    def bd_copy(way, j, p, peer, own_src):
        ss, rs = (fw_send, fw_recv) if way == 2 else (bd_send.at[way], bd_recv.at[way])
        return pltpu.make_async_remote_copy(
            src_ref=bd_own(p) if own_src else bd_slot(j, p), dst_ref=bd_slot(j, p),
            send_sem=ss.at[p], recv_sem=rs.at[p],
            device_id={"col": peer}, device_id_type=MESH)

    for p in range(PIECES):
        bd_copy(0, me, p, far, True).start()
    for k in range(AHEAD):
        send_own(k)
    for p in range(PIECES):
        bd_copy(1, me, p, sib, True).start()
    loads = [
        pltpu.make_async_copy(bd_ref, bd_all.at[pl.ds(pl.multiple_of(me * qc, qc), qc), :], load_sem.at[0]),
        pltpu.make_async_copy(ac_ref, ac_all.at[:, pl.ds(pl.multiple_of(z * qz, qz), qz)], load_sem.at[1]),
        pltpu.make_async_copy(t_ref, t_all, load_sem.at[2]),
    ]
    for copy in loads:
        copy.start()
    total[...] = jnp.zeros_like(total)

    def pump(h, k):
        @pl.when(z - 1 - h >= 0)
        def _():
            from_left(h, k).wait_recv()
            if h + 1 < hops:
                @pl.when(has_r)
                def _():
                    right(h + 1, k).start()

        @pl.when(z + 1 + h < nz)
        def _():
            from_right(h, k).wait_recv()
            if h + 1 < hops:
                @pl.when(has_l)
                def _():
                    left(h + 1, k).start()

    def compute(k):
        first = pl.multiple_of(k * rows, rows)
        c_in = rows // aw
        b_in = NT // dw

        def tile(n, carry):
            block = jnp.dot(
                ac_all[pl.ds(first, rows), :],
                bd_all[:, pl.ds(pl.multiple_of(n * NT, NT), NT)],
                preferred_element_type=jnp.float32,
            ).astype(jnp.bfloat16)
            for b in range(b_in):
                at = pl.multiple_of((n * b_in + b) * aw, aw)
                for c in range(c_in):
                    x_buf[pl.ds(at, aw), c * dw:(c + 1) * dw] = (
                        block[c * aw:(c + 1) * aw, b * dw:(b + 1) * dw])
            return carry

        lax.fori_loop(0, n_total // NT, tile, 0)
        kk = c_in * dw
        m = 256

        def add(i, carry):
            at = pl.ds(pl.multiple_of(i * m, m), m)
            total[at, :] += jnp.dot(
                x_buf[at, :], t_all[pl.ds(pl.multiple_of(k * kk, kk), kk), :],
                preferred_element_type=jnp.float32)
            return carry

        lax.fori_loop(0, total.shape[0] // m, add, 0)

    def step(s, carry):
        @pl.when(s + AHEAD < CHUNKS)
        def _():
            send_own(s + AHEAD)

        for h in range(hops):
            @pl.when((s >= h) & (s - h < CHUNKS))
            def _():
                pump(h, s - h)

        @pl.when(s == hops - 1)
        def _():
            for p in range(PIECES):
                bd_copy(0, far, p, far, False).wait_recv()
                bd_copy(2, far, p, sib, False).start()
            for p in range(PIECES):
                bd_copy(1, sib, p, sib, False).wait_recv()
            for p in range(PIECES):
                bd_copy(2, farsib, p, sib, False).wait_recv()
            for copy in loads:
                copy.wait()

        @pl.when(s >= hops - 1)
        def _():
            compute(s - (hops - 1))

        return carry

    lax.fori_loop(0, CHUNKS + hops - 1, step, 0)

    a_own = aw // 4
    bw = n_total // dw

    def place(b, carry):
        for a in range(4):
            out_ref[pl.ds(pl.multiple_of((a * bw + b) * a_own, a_own), a_own), :] = (
                total[pl.ds(pl.multiple_of(b * aw + a * a_own, a_own), a_own), :])
        return carry

    lax.fori_loop(0, bw, place, 0)

    for p in range(PIECES):
        bd_copy(0, me, p, far, True).wait_send()
        bd_copy(1, me, p, sib, True).wait_send()
        bd_copy(2, far, p, sib, False).wait_send()

    def drain(k, carry):
        for h in range(hops):
            @pl.when(has_r & (z - h >= 0))
            def _():
                right(h, k).wait_send()

            @pl.when(has_l & (z + h < nz))
            def _():
                left(h, k).wait_send()
        return carry

    lax.fori_loop(0, CHUNKS, drain, 0)


def fused(nz, factor_ac, factor_bd, amplitudes):
    qz, aw, cw = factor_ac.shape
    qc, bw, dw = factor_bd.shape
    npair = amplitudes.shape[2]
    rows_ac = factor_ac.transpose(2, 1, 0).reshape(cw * aw, qz)
    rows_bd = factor_bd.reshape(qc, bw * dw)
    rows_t = amplitudes.reshape(cw * dw, npair)
    hops = nz - 1
    dma = pltpu.SemaphoreType.DMA
    any_space = pl.BlockSpec(memory_space=pl.ANY)
    partial_sum = pl.pallas_call(
        functools.partial(kernel, nz, aw, dw, cw),
        out_shape=jax.ShapeDtypeStruct((bw * aw, npair), jnp.float32),
        in_specs=[any_space] * 3,
        out_specs=pl.BlockSpec(memory_space=pltpu.VMEM),
        scratch_shapes=[
            pltpu.VMEM((cw * aw, nz * qz), jnp.bfloat16),
            pltpu.VMEM((4 * qc, bw * dw), jnp.bfloat16),
            pltpu.VMEM((cw * dw, npair), jnp.bfloat16),
            pltpu.VMEM((bw * aw, cw // CHUNKS * dw), jnp.bfloat16),
            pltpu.VMEM((bw * aw, npair), jnp.float32),
            dma((3,)), dma((2, PIECES)), dma((2, PIECES)), dma((PIECES,)), dma((PIECES,)),
            dma((hops, CHUNKS)), dma((hops, CHUNKS)), dma((hops, CHUNKS)), dma((hops, CHUNKS)),
        ],
        compiler_params=pltpu.CompilerParams(
            collective_id=0, has_side_effects=True, vmem_limit_bytes=58 * 2 ** 20),
    )(rows_ac, rows_bd, rows_t)
    blocks = partial_sum.reshape(4 * nz, bw // nz, aw // 4, npair)
    result = lax.all_to_all(blocks, ("col", "dev"), 0, 0, tiled=True).sum(0)
    return result.transpose(1, 0, 2)


def gathered(factor_ac, factor_bd, amplitudes):
    whole_bd = lax.all_gather(factor_bd, "col", axis=0, tiled=True)
    whole_ac = lax.all_gather(factor_ac, "dev", axis=0, tiled=True)
    integral = jnp.einsum("qac,qbd->abdc", whole_ac, whole_bd, preferred_element_type=jnp.float32)
    integral = integral.astype(jnp.bfloat16)
    partial_sum = jnp.einsum(
        "abdc,cdp->abp", integral, amplitudes, preferred_element_type=jnp.float32
    )
    reduced = lax.psum_scatter(partial_sum, "col", scatter_dimension=0, tiled=True)
    return lax.psum_scatter(reduced, "dev", scatter_dimension=1, tiled=True)


def solution(mesh):
    nz, ncol = mesh.shape["dev"], mesh.shape["col"]

    def local(factor_ac, factor_bd, amplitudes):
        qz, aw, cw = factor_ac.shape
        qc, bw, dw = factor_bd.shape
        held = 2 * (cw * aw * nz * qz + ncol * qc * bw * dw + cw * dw * amplitudes.shape[2])
        fits = (ncol == 4 and 2 <= nz and dw == 128 and qz % 128 == 0 and qc % (16 * PIECES) == 0
                and aw % 32 == 0 and bw % nz == 0 and cw % CHUNKS == 0 and bw * dw % NT == 0
                and bw * aw % 256 == 0 and CHUNKS >= AHEAD and held <= 36 * 2 ** 20)
        if fits:
            return fused(nz, factor_ac, factor_bd, amplitudes)
        return gathered(factor_ac, factor_bd, amplitudes)

    placed = (
        P(("frag", "dev"), None, "col"),
        P(("frag", "col"), None, "dev"),
        P(("frag", "col"), "dev", None),
    )
    return jax.shard_map(
        local,
        mesh=mesh,
        in_specs=placed,
        out_specs=P(("frag", "col"), "dev", None),
        check_vma=False,
    )
```
